128 devices in a mesh: day: 32 (over z, x, core), pt: 4 (over y).
Axes of the slice: x: 4, y: 4, z: 4, core: 2. Of those that a mesh axis runs over, the one named last changes fastest.
Arguments:
- points: bfloat16 [32, 64, 2048], P('day', None, 'pt'), may hold values from -0.45 to 0.45
- cells: bfloat16 [32, 64, 8192], P('day', None, 'pt'), may hold values from -0.44921875 to 0.44921875
- clone_weight: float32 [32, 64, 2048], P('day', None, 'pt'), may hold values from 0.1 to 1
- potential: float32 [32, 2048], P('day', 'pt'), may hold values from 0.2 to 5
- support_count: int32 [32], P('day'), may hold values from 512 to 2048, as said below
- cell_count: int32 [32], P('day'), may hold values from 2048 to 8192, as said below
Outputs:
- forward_message: float32 [32, 64, 2048], P('day', None, 'pt')
- backward_message: float32 [32, 64, 2048], P('day', None, 'pt')
- fit_ratio: float32 [32, 2048], P('day', 'pt')
The draws below stay inside these ranges and needn't reach their ends.
Inputs may be any that keep to these rules, and one draw needn't show every extreme that they name: Live support points of a day are its first support_count slots; some day has all 2048 slots live and some day has 512. Observed cells of a day are its first cell_count slots; some day fills all 8192 slots and some day has 2048.
All inputs are finite; a program needn't handle non-finite values.
Results may differ from the reference program's by a relative error of at most 0.0003.
Values may be sent and summed in bfloat16 or wider, within the bound.
A program may use at most 64 MiB of HBM per device.

```python
import jax
import jax.numpy as jnp
from jax import lax

D = 64
C = 64
DAYS = 32
PTS = 2048
OBS = 8192


def pick_counts(key, slots):
    first_key, second_key = jax.random.split(key)
    drawn = jax.random.randint(first_key, (DAYS,), slots // 4, slots + 1)
    order = jax.random.permutation(second_key, DAYS)
    drawn = drawn.at[order[0]].set(slots)
    drawn = drawn.at[order[1]].set(slots // 4)
    return drawn.astype(jnp.int32)


def draw_support_count(key, part):
    return pick_counts(jax.random.fold_in(key, 11), PTS)


def draw_cell_count(key, part):
    return pick_counts(jax.random.fold_in(key, 23), OBS)


def slot_parity():
    return (jnp.arange(PTS, dtype=jnp.int32) % 2).astype(jnp.float32)


def draw_points(key, part):
    jitter_key = jax.random.fold_in(key, 37)
    cluster_sign = 1.0 - 2.0 * slot_parity()
    jitter = 0.08 * jnp.clip(jax.random.normal(jitter_key, (DAYS, D, PTS), jnp.float32), -3.0, 3.0)
    centre = 0.2
    values = centre * cluster_sign[None, None, :] + jitter
    return jnp.clip(values, -0.45, 0.45).astype(jnp.bfloat16)


def draw_clone_weight(key, part):
    cluster_key = jax.random.fold_in(key, 41)
    entry_key = jax.random.fold_in(key, 43)
    parity = slot_parity()
    grouped = jax.random.uniform(cluster_key, (DAYS, C, 2), jnp.float32)
    entries = jax.random.uniform(entry_key, (DAYS, C, PTS), jnp.float32)
    chosen = grouped[:, :, 0:1] * (1.0 - parity)[None, None, :] + grouped[:, :, 1:2] * parity[None, None, :]
    exponent = -1.0 + 0.4 * chosen + 0.6 * entries
    return jnp.exp(exponent * 2.302585093).astype(jnp.float32)


def draw_potential(key, part):
    cluster_key = jax.random.fold_in(key, 47)
    entry_key = jax.random.fold_in(key, 53)
    parity = slot_parity()
    grouped = jax.random.uniform(cluster_key, (DAYS, 2), jnp.float32, -1.0, 1.0)
    entries = jax.random.uniform(entry_key, (DAYS, PTS), jnp.float32, -1.0, 1.0)
    chosen = grouped[:, 0:1] * (1.0 - parity)[None, :] + grouped[:, 1:2] * parity[None, :]
    exponent = 0.6 * chosen + 0.8 * entries
    return jnp.exp(exponent).astype(jnp.float32)


def levels(rng, shape, pieces, least, top_value):
    def one(dim, blocks):
        heights = jax.random.uniform(jax.random.fold_in(jax.random.fold_in(rng, 6), dim), (blocks,), jnp.float32, least / len(pieces), top_value / len(pieces))
        return jnp.repeat(jnp.exp(heights), shape[dim] // blocks).reshape((-1,) + (1,) * (len(shape) - dim - 1))

    factor_of = one(*pieces[0])
    for cut in pieces[1:]:
        factor_of = factor_of * one(*cut)
    return factor_of


def setup_inputs(seed: int = 0) -> dict:
    streams_of = jax.random.split(jax.random.key(seed), 7)
    return {
        "points": draw_points(jax.random.fold_in(streams_of[6], 71), 0),
        "cells": jnp.clip(jax.random.uniform(streams_of[1], (DAYS, D, OBS), jnp.float32, -0.44921875, 0.44921875) * levels(streams_of[1], (DAYS, D, OBS), ((0, 32), (2, 4)), -0.4, 0.0), -0.44921875, 0.44921875).astype(jnp.bfloat16),
        "clone_weight": draw_clone_weight(jax.random.fold_in(streams_of[6], 71), 0),
        "potential": draw_potential(jax.random.fold_in(streams_of[6], 71), 0),
        "support_count": draw_support_count(jax.random.fold_in(streams_of[6], 71), 0),
        "cell_count": draw_cell_count(jax.random.fold_in(streams_of[6], 71), 0),
    }


def squared_dist(left_pts, right_pts):
    left_wide = left_pts.astype(jnp.float32)
    right_wide = right_pts.astype(jnp.float32)
    left_norm = jnp.sum(left_wide * left_wide, axis=0)
    right_norm = jnp.sum(right_wide * right_wide, axis=0)
    inner = lax.dot_general(left_pts, right_pts, (((0,), (0,)), ((), ())), preferred_element_type=jnp.float32)
    return left_norm[:, None] + right_norm[None, :] - 2.0 * inner


def settle(values, live_next, day_total):
    masked = values * live_next[None, :]
    return masked * day_total / jnp.sum(masked, axis=1, keepdims=True)


def advance(message, inputs):
    source_pts, target_pts, source_weight, live_next, day_total = inputs
    sent_rows = (message * source_weight).astype(jnp.bfloat16)
    chain_kernel = jnp.exp(-squared_dist(source_pts, target_pts)).astype(jnp.bfloat16)
    advanced = settle(jnp.dot(sent_rows, chain_kernel, preferred_element_type=jnp.float32), live_next, day_total)
    return advanced, advanced


def reference(points, cells, clone_weight, potential, support_count, cell_count):
    support_total = points.shape[2]
    cell_slots = cells.shape[2]
    clones = clone_weight.shape[1]
    positions = jnp.arange(support_total, dtype=jnp.int32)
    live_rows = (positions[None, :] < support_count[:, None]).astype(jnp.float32)
    weight = clone_weight * potential[:, None, :]
    day_totals = support_count.astype(jnp.float32)
    first_message = jnp.broadcast_to(live_rows[0][None, :], (clones, support_total))
    ignored, later = lax.scan(advance, first_message, (points[:-1], points[1:], weight[:-1], live_rows[1:], day_totals[1:]))
    forward_message = jnp.concatenate([first_message[None], later], axis=0)
    final_message = jnp.broadcast_to(live_rows[-1][None, :], (clones, support_total))
    ignored_too, earlier = lax.scan(advance, final_message, (points[1:], points[:-1], weight[1:], live_rows[:-1], day_totals[:-1]), reverse=True)
    backward_message = jnp.concatenate([earlier, final_message[None]], axis=0)
    mass_rows = live_rows * potential * jnp.sum(forward_message * clone_weight * backward_message, axis=1)

    def fit_day(inputs):
        day_pts, day_cells, day_mass, day_live, cell_total = inputs
        fit_kernel = jnp.exp(-squared_dist(day_pts, day_cells))
        density = jnp.dot(day_mass, fit_kernel, precision=lax.Precision.HIGHEST) / jnp.sum(day_mass)
        cell_live = (jnp.arange(cell_slots, dtype=jnp.int32) < cell_total).astype(jnp.float32)
        summed = jnp.dot(fit_kernel, cell_live / density, precision=lax.Precision.HIGHEST)
        return day_live / cell_total.astype(jnp.float32) * summed

    fit_ratio = lax.map(fit_day, (points, cells, mass_rows, live_rows, cell_count))
    return forward_message, backward_message, fit_ratio
```

```python
import jax
import jax.numpy as jnp
from jax import lax
from jax.experimental import pallas as pl
from jax.experimental.pallas import tpu as pltpu
from jax.sharding import PartitionSpec as P

MESH = pl.DeviceIdType.MESH
F32 = jnp.float32
BF16 = jnp.bfloat16
TEAMS = 8
GROUPS = 8
DEPTH = 80
ROWS = 256


def remote(src, dst, send_sem, recv_sem, day, pt):
    return pltpu.make_async_remote_copy(
        src_ref=src,
        dst_ref=dst,
        send_sem=send_sem,
        recv_sem=recv_sem,
        device_id=(day, pt),
        device_id_type=MESH,
    )


def parts_of(norm):
    first = norm.astype(BF16).astype(F32)
    rest = norm - first
    second = rest.astype(BF16).astype(F32)
    third = (rest - second).astype(BF16).astype(F32)
    return first, second, third


def fill_side(side, coords, factor, norms_first):
    wide = coords.astype(F32)
    norm = -jnp.sum(wide * wide, axis=0, keepdims=True)
    one, two, three = parts_of(norm)
    shape = (DEPTH - 64, coords.shape[1])
    row = lax.broadcasted_iota(jnp.int32, shape, 0)
    if not norms_first:
        row = jnp.where(row < 3, row + 3, jnp.where(row < 6, row - 3, row))
    extra = jnp.where(row == 0, one, jnp.where(row == 1, two, jnp.where(row == 2, three, 0.0)))
    extra = jnp.where((row >= 3) & (row < 6), 1.0, extra)
    side[0:64, :] = (wide * factor).astype(BF16)
    side[64:DEPTH, :] = extra.astype(BF16)


def body(
    pts_in, cells_in, cw_in, pot_in, sc_in, cc_in, fb_out, fit_out,
    kern, fit, pts, wts, res, oth, msg, wsrc, left, right, mps, mbuf, mrow, rpart, rbuf,
    rs_p, rs_w, ss_p, ss_w, ss_i, ss_f, ss_g, rs_u, ss_u, rs_o, ss_o, rs_x, ss_x, rs_m, ss_m,
    rs_r, ss_r,
):
    d = lax.axis_index("day")
    p = lax.axis_index("pt")
    q = d // 4
    dl = d % 4
    core = d % 2
    pair = q % 2
    xb = (d // 2) % 2
    bit = jnp.where(pair == 0, xb, 1 - xb)
    g = 2 * p + bit
    early = core == 1
    low = q < TEAMS // 2
    fwd = early == low
    stage = jnp.where(fwd, q, TEAMS - 1 - q)
    starts = stage == 0
    own_col = pl.multiple_of(p * 512, 512)

    def day_at(place):
        return 4 * q + jnp.where(fwd, place - 1, 4 - place)

    def chain_day(team, group, at_core):
        flip = team % 2
        side = group % 2
        return 4 * team + 2 * jnp.where(flip == 0, side, 1 - side) + at_core

    barrier = pltpu.get_barrier_semaphore()

    def greet(n, carry):
        team = q - 1 + n // 16
        day = 4 * team + (n % 16) // 4
        pt = n % 4
        ok = (team >= 0) & (team < TEAMS) & jnp.logical_not((day == d) & (pt == p))

        @pl.when(ok)
        def _():
            pl.semaphore_signal(barrier, inc=1, device_id=(day, pt), device_id_type=MESH)

        return carry

    lax.fori_loop(0, 48, greet, 0)

    slot_own = lax.broadcasted_iota(jnp.int32, (1, 512), 1) + p * 512
    live_own = (slot_own < sc_in[0]).astype(F32)
    wsrc[...] = cw_in[0] * (pot_in[...] * live_own)

    others = 15 + jnp.where(q > 0, 16, 0) + jnp.where(q < TEAMS - 1, 16, 0)
    pl.semaphore_wait(barrier, others)

    place_own = jnp.where(low, dl + 1, 4 - dl)

    def pts_copy(group, team, at_core, place, send_sem):
        return remote(
            pts_in.at[0],
            pts.at[place, :, pl.ds(own_col, 512)],
            send_sem,
            rs_p.at[place, p],
            chain_day(team, group, at_core),
            group // 2,
        )

    def wts_copy(group):
        return remote(
            wsrc.at[pl.ds(pl.multiple_of(8 * group, 8), 8), :],
            wts.at[place_own - 1, :, pl.ds(own_col, 512)],
            ss_w.at[group],
            rs_w.at[place_own - 1, p],
            chain_day(q, group, 1),
            group // 2,
        )

    def is_self(group):
        return (chain_day(q, group, 1) == d) & (group // 2 == p)

    def give(group, carry):
        @pl.when(is_self(group))
        def _():
            pltpu.make_async_copy(
                pts_in.at[0], pts.at[place_own, :, pl.ds(own_col, 512)], rs_p.at[place_own, p]
            ).start()
            pltpu.make_async_copy(
                wsrc.at[pl.ds(pl.multiple_of(8 * group, 8), 8), :],
                wts.at[place_own - 1, :, pl.ds(own_col, 512)],
                rs_w.at[place_own - 1, p],
            ).start()

        @pl.when(jnp.logical_not(is_self(group)))
        def _():
            pts_copy(group, q, 1, place_own, ss_p.at[group]).start()
            wts_copy(group).start()

        return carry

    lax.fori_loop(0, GROUPS, give, 0)

    to_next = (dl == 3) & (q < TEAMS - 1)
    to_last = (dl == 0) & (q > 0)
    side_team = jnp.where(dl == 3, q + 1, q - 1)
    side_core = jnp.where(
        dl == 3,
        jnp.where(side_team < TEAMS // 2, 1, 0),
        jnp.where(side_team < TEAMS // 2, 0, 1),
    )

    def side_copy(group):
        return pts_copy(group, side_team, side_core, 0, ss_i.at[group])

    @pl.when(to_next | to_last)
    def _():
        def give_side(group, carry):
            side_copy(group).start()
            return carry

        lax.fori_loop(0, GROUPS, give_side, 0)

    mate = d - 1

    def pts_pass(place):
        return remote(
            pts.at[place], pts.at[5 - place], ss_f.at[place - 1], rs_p.at[5 - place, 0], mate, p
        )

    def wts_pass(index):
        return remote(
            wts.at[index], wts.at[3 - index], ss_g.at[index], rs_w.at[3 - index, 0], mate, p
        )

    def wait_blocks(place):
        def one(k, carry):
            dst = pts.at[place, :, pl.ds(pl.multiple_of(k * 512, 512), 512)]
            remote(pts_in.at[0], dst, ss_u, rs_p.at[place, k], d, p).wait_recv()
            return carry

        lax.fori_loop(0, 4, one, 0)

    def take_day(place):
        @pl.when(early)
        def _():
            wait_blocks(place)
            pts_pass(place).start()

            def one(k, carry):
                dst = wts.at[place - 1, :, pl.ds(pl.multiple_of(k * 512, 512), 512)]
                src = wsrc.at[pl.ds(0, 8), :]
                remote(src, dst, ss_u, rs_w.at[place - 1, k], d, p).wait_recv()
                return carry

            lax.fori_loop(0, 4, one, 0)
            wts_pass(place - 1).start()

        @pl.when(jnp.logical_not(early))
        def _():
            remote(
                pts.at[place], pts.at[place], ss_u, rs_p.at[place, 0], d, p
            ).wait_recv()
            remote(
                wts.at[place - 1], wts.at[place - 1], ss_u, rs_w.at[place - 1, 0], d, p
            ).wait_recv()

    def send_form(values):
        return jnp.concatenate([values[:, 0:1024], values[:, 1024:2048]], axis=0).astype(BF16)

    def step(index):
        low_part = jnp.dot(msg[...], kern[index, 0:1024, :], preferred_element_type=F32)
        high_part = jnp.dot(msg[...], kern[index, 1024:2048, :], preferred_element_type=F32)
        weight = wts[index]
        live = (weight > 0.0).astype(F32)
        count = jnp.sum(live, axis=1, keepdims=True)
        masked = (low_part[0:8] + high_part[8:16]) * live
        settled = masked * (count / jnp.sum(masked, axis=1, keepdims=True))
        msg[...] = send_form(settled * weight)
        res[index] = settled

    take_day(1)

    @pl.when(starts)
    def _():
        weight = wts[0]
        live = (weight > 0.0).astype(F32)
        res[0] = live
        msg[...] = send_form(live * weight)

    def make_kernel(t, carry):
        index = (t + 1) % 4

        @pl.when(index > 0)
        def _():
            take_day(index + 1)

        @pl.when((index > 0) | jnp.logical_not(starts))
        def _():
            @pl.when(index == 0)
            def _():
                wait_blocks(0)

            fill_side(left, pts[index], 1.0, True)
            fill_side(right, pts[index + 1], 2.0, False)

            def rows(r, inner):
                at = pl.ds(pl.multiple_of(r * ROWS, ROWS), ROWS)
                power = lax.dot_general(
                    left[:, at], right[...], (((0,), (0,)), ((), ())), preferred_element_type=F32
                )
                kern[index, at, :] = jnp.exp(power).astype(BF16)
                return inner

            lax.fori_loop(0, 2048 // ROWS, rows, 0)

        @pl.when((index > 0) & starts)
        def _():
            step(index)

        return carry

    lax.fori_loop(0, 4, make_kernel, 0)

    def make_fit():
        fill_side(left, pts[jnp.where(fwd, dl + 1, 4 - dl)], 1.0, True)
        fill_side(right, cells_in[0], 2.0, False)

        def rows(r, inner):
            at = pl.ds(pl.multiple_of(r * ROWS, ROWS), ROWS)
            power = lax.dot_general(
                left[:, at], right[...], (((0,), (0,)), ((), ())), preferred_element_type=F32
            )
            fit[at, :] = jnp.exp(power)
            return inner

        lax.fori_loop(0, 2048 // ROWS, rows, 0)

    next_team = jnp.where(fwd, q + 1, q - 1)
    next_core = jnp.where(fwd == (next_team < TEAMS // 2), 1, 0)
    next_day = 4 * next_team + 2 * (1 - xb) + next_core
    hop = remote(msg, msg, ss_u, rs_u, next_day, p)

    def cross(index):
        return remote(res.at[index], oth.at[3 - index], ss_x.at[index], rs_x.at[3 - index], mate, p)

    @pl.when(jnp.logical_not(early))
    def _():
        make_fit()

    @pl.when(jnp.logical_not(starts))
    def _():
        remote(msg, msg, ss_u, rs_u, d, p).wait_recv()

        def one(index, carry):
            step(index)
            return carry

        lax.fori_loop(0, 4, one, 0)

    @pl.when(stage < TEAMS - 1)
    def _():
        hop.start()

    def mass_copy(index, k):
        return remote(
            mps.at[index], mbuf.at[g], ss_m.at[index, k], rs_m.at[g], day_at(index + 1), k
        )

    def here(index, k):
        return (day_at(index + 1) == d) & (k == p)

    @pl.when(jnp.logical_not(early))
    def _():
        def one(t, carry):
            index = 3 - t
            remote(res.at[index], oth.at[index], ss_u, rs_x.at[index], d, p).wait_recv()
            mps[index] = jnp.sum(res[index] * wts[index] * oth[index], axis=0, keepdims=True)

            def to(k, inner):
                @pl.when(here(index, k))
                def _():
                    pltpu.make_async_copy(mps.at[index], mbuf.at[g], rs_m.at[g]).start()

                @pl.when(jnp.logical_not(here(index, k)))
                def _():
                    mass_copy(index, k).start()

                return inner

            lax.fori_loop(0, 4, to, 0)
            return carry

        lax.fori_loop(0, 4, one, 0)

    @pl.when(early)
    def _():
        def one(index, carry):
            cross(index).start()
            return carry

        lax.fori_loop(0, 4, one, 0)

    way = jnp.where(fwd, 0, 1)
    rows_g = pl.ds(pl.multiple_of(8 * g, 8), 8)

    def out_copy(index, k):
        return remote(
            res.at[index, :, pl.ds(pl.multiple_of(k * 512, 512), 512)],
            fb_out.at[way, rows_g, :],
            ss_o.at[index, k],
            rs_o.at[way, g],
            day_at(index + 1),
            k,
        )

    def out_days(index, carry):
        def to(k, inner):
            @pl.when(here(index, k))
            def _():
                pltpu.make_async_copy(
                    res.at[index, :, pl.ds(pl.multiple_of(k * 512, 512), 512)],
                    fb_out.at[way, rows_g, :],
                    rs_o.at[way, g],
                ).start()

            @pl.when(jnp.logical_not(here(index, k)))
            def _():
                out_copy(index, k).start()

            return inner

        lax.fori_loop(0, 4, to, 0)
        return carry

    lax.fori_loop(0, 4, out_days, 0)

    @pl.when(early)
    def _():
        make_fit()

    def wait_mass(k, carry):
        remote(mps.at[0], mbuf.at[k], ss_u, rs_m.at[k], d, p).wait_recv()
        return carry

    lax.fori_loop(0, GROUPS, wait_mass, 0)
    mass = mbuf[0]
    for k in range(1, GROUPS):
        mass = mass + mbuf[k]
    mass_total = jnp.sum(mass, axis=1, keepdims=True)
    mrow[...] = jnp.zeros_like(mrow)
    for k in range(16):
        mrow[k : k + 1, :] = mass[:, 128 * k : 128 * k + 128]
    columns = jnp.transpose(mrow[...])
    total = jnp.zeros((8, 2048), F32)
    for k in range(16):
        block = fit[128 * k : 128 * k + 128, :] * columns[:, k : k + 1]
        total = total + jnp.sum(block.reshape(16, 8, 2048), axis=0)
    density = jnp.sum(total, axis=0, keepdims=True) / mass_total
    cell = lax.broadcasted_iota(jnp.int32, (1, 2048), 1) + p * 2048
    inverse = (cell < cc_in[0]).astype(F32) / density
    for k in range(16):
        part = jnp.zeros((128, 128), F32)
        for c in range(16):
            part = part + (
                fit[128 * k : 128 * k + 128, 128 * c : 128 * c + 128]
                * inverse[:, 128 * c : 128 * c + 128]
            )
        rpart[k // 4, :, 128 * (k % 4) : 128 * (k % 4) + 128] = jnp.sum(
            jnp.transpose(part), axis=0, keepdims=True
        )

    def ratio_copy(k):
        return remote(rpart.at[k], rbuf.at[p], ss_r.at[k], rs_r.at[p], d, k)

    def ratio_to(k, carry):
        @pl.when(k == p)
        def _():
            pltpu.make_async_copy(rpart.at[k], rbuf.at[p], rs_r.at[p]).start()

        @pl.when(k != p)
        def _():
            ratio_copy(k).start()

        return carry

    lax.fori_loop(0, 4, ratio_to, 0)

    def ratio_wait(k, carry):
        remote(rpart.at[0], rbuf.at[k], ss_u, rs_r.at[k], d, p).wait_recv()
        return carry

    lax.fori_loop(0, 4, ratio_wait, 0)
    summed = rbuf[0] + rbuf[1] + rbuf[2] + rbuf[3]
    fit_out[...] = live_own / jnp.full((1, 512), cc_in[0], jnp.int32).astype(F32) * summed

    def close_give(group, carry):
        @pl.when(jnp.logical_not(is_self(group)))
        def _():
            pts_copy(group, q, 1, place_own, ss_p.at[group]).wait_send()
            wts_copy(group).wait_send()

        @pl.when(to_next | to_last)
        def _():
            side_copy(group).wait_send()

        def arrived(way_in, inner):
            remote(
                res.at[0, :, pl.ds(0, 512)],
                fb_out.at[way_in, pl.ds(pl.multiple_of(8 * group, 8), 8), :],
                ss_u,
                rs_o.at[way_in, group],
                d,
                p,
            ).wait_recv()
            return inner

        lax.fori_loop(0, 2, arrived, 0)
        return carry

    lax.fori_loop(0, GROUPS, close_give, 0)

    def close_four(index, carry):
        @pl.when(early)
        def _():
            pts_pass(index + 1).wait_send()
            wts_pass(index).wait_send()
            cross(index).wait_send()

        @pl.when(index != p)
        def _():
            ratio_copy(index).wait_send()

        def to(k, inner):
            @pl.when(jnp.logical_not(here(index, k)))
            def _():
                out_copy(index, k).wait_send()

                @pl.when(jnp.logical_not(early))
                def _():
                    mass_copy(index, k).wait_send()

            return inner

        lax.fori_loop(0, 4, to, 0)
        return carry

    lax.fori_loop(0, 4, close_four, 0)

    @pl.when(stage < TEAMS - 1)
    def _():
        hop.wait_send()


def shards(points, cells, clone_weight, potential, support_count, cell_count):
    vmem = pl.BlockSpec(memory_space=pltpu.VMEM)
    smem = pl.BlockSpec(memory_space=pltpu.SMEM)
    dma = pltpu.SemaphoreType.DMA
    both, ratio = pl.pallas_call(
        body,
        out_shape=(
            jax.ShapeDtypeStruct((2, 64, 512), F32),
            jax.ShapeDtypeStruct((1, 512), F32),
        ),
        in_specs=[vmem, vmem, vmem, vmem, smem, smem],
        out_specs=(pl.BlockSpec(memory_space=pl.ANY), vmem),
        scratch_shapes=[
            pltpu.VMEM((4, 2048, 2048), BF16),
            pltpu.VMEM((2048, 2048), F32),
            pltpu.VMEM((5, 64, 2048), BF16),
            pltpu.VMEM((4, 8, 2048), F32),
            pltpu.VMEM((4, 8, 2048), F32),
            pltpu.VMEM((4, 8, 2048), F32),
            pltpu.VMEM((16, 1024), BF16),
            pltpu.VMEM((64, 512), F32),
            pltpu.VMEM((DEPTH, 2048), BF16),
            pltpu.VMEM((DEPTH, 2048), BF16),
            pltpu.VMEM((4, 1, 2048), F32),
            pltpu.VMEM((GROUPS, 1, 2048), F32),
            pltpu.VMEM((128, 128), F32),
            pltpu.VMEM((4, 1, 512), F32),
            pltpu.VMEM((4, 1, 512), F32),
            dma((5, 4)),
            dma((4, 4)),
            dma((GROUPS,)),
            dma((GROUPS,)),
            dma((GROUPS,)),
            dma((4,)),
            dma((4,)),
            dma,
            dma,
            dma((2, GROUPS)),
            dma((4, 4)),
            dma((4,)),
            dma((4,)),
            dma((GROUPS,)),
            dma((4, 4)),
            dma((4,)),
            dma((4,)),
        ],
        compiler_params=pltpu.CompilerParams(
            collective_id=0, has_side_effects=True, vmem_limit_bytes=58 * 1024 * 1024
        ),
        name="days",
    )(points, cells, clone_weight, potential, support_count, cell_count)
    return both[0][None], both[1][None], ratio


def solution(mesh):
    in_specs = (
        P("day", None, "pt"),
        P("day", None, "pt"),
        P("day", None, "pt"),
        P("day", "pt"),
        P("day"),
        P("day"),
    )
    out_specs = (P("day", None, "pt"), P("day", None, "pt"), P("day", "pt"))
    return jax.shard_map(shards, mesh=mesh, in_specs=in_specs, out_specs=out_specs, check_vma=False)
```

```python
import jax
import jax.numpy as jnp
from jax import lax
from jax.experimental import pallas as pl
from jax.experimental.pallas import tpu as pltpu
from jax.sharding import PartitionSpec as P

MESH = pl.DeviceIdType.MESH
F32 = jnp.float32
BF16 = jnp.bfloat16
TEAMS = 8
GROUPS = 8
DEPTH = 80
ROWS = 512
ROWS_SUMMED = 512


def remote(src, dst, send_sem, recv_sem, day, pt):
    return pltpu.make_async_remote_copy(
        src_ref=src,
        dst_ref=dst,
        send_sem=send_sem,
        recv_sem=recv_sem,
        device_id=(day, pt),
        device_id_type=MESH,
    )


def parts_of(norm):
    first = norm.astype(BF16).astype(F32)
    rest = norm - first
    second = rest.astype(BF16).astype(F32)
    third = (rest - second).astype(BF16).astype(F32)
    return first, second, third


def fill_side(side, coords, factor, norms_first):
    wide = coords.astype(F32)
    norm = -jnp.sum(wide * wide, axis=0, keepdims=True)
    one, two, three = parts_of(norm)
    shape = (DEPTH - 64, coords.shape[1])
    row = lax.broadcasted_iota(jnp.int32, shape, 0)
    if not norms_first:
        row = jnp.where(row < 3, row + 3, jnp.where(row < 6, row - 3, row))
    extra = jnp.where(row == 0, one, jnp.where(row == 1, two, jnp.where(row == 2, three, 0.0)))
    extra = jnp.where((row >= 3) & (row < 6), 1.0, extra)
    side[0:64, :] = (wide * factor).astype(BF16)
    side[64:DEPTH, :] = extra.astype(BF16)


def body(
    pts_in, cells_in, cw_in, pot_in, sc_in, cc_in, fb_out, fit_out,
    kern, rsum, fit, pts, wts, res, oth, msg, wsrc, left, right, mps, mbuf, mrow, rpart, rbuf,
    rs_p, rs_w, ss_p, ss_w, ss_i, ss_f, ss_g, rs_u, ss_u, rs_o, ss_o, rs_x, ss_x, rs_m, ss_m,
    rs_r, ss_r,
):
    d = lax.axis_index("day")
    p = lax.axis_index("pt")
    q = d // 4
    dl = d % 4
    core = d % 2
    pair = q % 2
    xb = (d // 2) % 2
    bit = jnp.where(pair == 0, xb, 1 - xb)
    g = 2 * p + bit
    early = core == 1
    low = q < TEAMS // 2
    fwd = early == low
    stage = jnp.where(fwd, q, TEAMS - 1 - q)
    starts = stage == 0
    own_col = pl.multiple_of(p * 512, 512)

    def day_at(place):
        return 4 * q + jnp.where(fwd, place - 1, 4 - place)

    def chain_day(team, group, at_core):
        flip = team % 2
        side = group % 2
        return 4 * team + 2 * jnp.where(flip == 0, side, 1 - side) + at_core

    barrier = pltpu.get_barrier_semaphore()

    def greet(n, carry):
        day = 4 * q + n // 4
        pt = n % 4

        @pl.when(jnp.logical_not((day == d) & (pt == p)))
        def _():
            pl.semaphore_signal(barrier, inc=1, device_id=(day, pt), device_id_type=MESH)

        return carry

    lax.fori_loop(0, 16, greet, 0)

    @pl.when(jnp.logical_not(starts))
    def _():
        last_team = jnp.where(fwd, q - 1, q + 1)
        last_core = jnp.where(fwd == (last_team < TEAMS // 2), 1, 0)
        last_day = 4 * last_team + 2 * (1 - xb) + last_core
        pl.semaphore_signal(barrier, inc=1, device_id=(last_day, p), device_id_type=MESH)

        def greet_side(pt, carry):
            day = jnp.where(fwd, 4 * q - 1, 4 * q + 4)
            pl.semaphore_signal(barrier, inc=1, device_id=(day, pt), device_id_type=MESH)
            return carry

        lax.fori_loop(0, 4, greet_side, 0)

    slot_own = lax.broadcasted_iota(jnp.int32, (1, 512), 1) + p * 512
    live_own = (slot_own < sc_in[0]).astype(F32)
    wsrc[...] = cw_in[0] * (pot_in[...] * live_own)

    to_next = (dl == 3) & (q < TEAMS - 1)
    to_last = (dl == 0) & (q > 0)
    others = 15 + jnp.where(to_next | to_last, GROUPS, 0) + jnp.where(stage < TEAMS - 1, 1, 0)
    pl.semaphore_wait(barrier, others)

    place_own = jnp.where(low, dl + 1, 4 - dl)

    def pts_copy(group, team, at_core, place, send_sem):
        return remote(
            pts_in.at[0],
            pts.at[place, :, pl.ds(own_col, 512)],
            send_sem,
            rs_p.at[place, p],
            chain_day(team, group, at_core),
            group // 2,
        )

    def wts_copy(group):
        return remote(
            wsrc.at[pl.ds(pl.multiple_of(8 * group, 8), 8), :],
            wts.at[place_own - 1, :, pl.ds(own_col, 512)],
            ss_w.at[group],
            rs_w.at[place_own - 1, p],
            chain_day(q, group, 1),
            group // 2,
        )

    def is_self(group):
        return (chain_day(q, group, 1) == d) & (group // 2 == p)

    def give_pts(group, carry):
        @pl.when(is_self(group))
        def _():
            pltpu.make_async_copy(
                pts_in.at[0], pts.at[place_own, :, pl.ds(own_col, 512)], rs_p.at[place_own, p]
            ).start()

        @pl.when(jnp.logical_not(is_self(group)))
        def _():
            pts_copy(group, q, 1, place_own, ss_p.at[group]).start()

        return carry

    def give_wts(group, carry):
        @pl.when(is_self(group))
        def _():
            pltpu.make_async_copy(
                wsrc.at[pl.ds(pl.multiple_of(8 * group, 8), 8), :],
                wts.at[place_own - 1, :, pl.ds(own_col, 512)],
                rs_w.at[place_own - 1, p],
            ).start()

        @pl.when(jnp.logical_not(is_self(group)))
        def _():
            wts_copy(group).start()

        return carry

    def give():
        def turned(group):
            return lax.rem(group + 2 * p + 2, GROUPS)

        lax.fori_loop(0, GROUPS, lambda n, carry: give_pts(turned(n), carry), 0)
        lax.fori_loop(0, GROUPS, lambda n, carry: give_wts(turned(n), carry), 0)

    give()

    side_team = jnp.where(dl == 3, q + 1, q - 1)
    side_core = jnp.where(
        dl == 3,
        jnp.where(side_team < TEAMS // 2, 1, 0),
        jnp.where(side_team < TEAMS // 2, 0, 1),
    )

    def side_copy(group):
        return pts_copy(group, side_team, side_core, 0, ss_i.at[group])

    mate = d - 1

    def pts_pass(place):
        return remote(
            pts.at[place], pts.at[5 - place], ss_f.at[place - 1], rs_p.at[5 - place, 0], mate, p
        )

    def wts_pass(index):
        return remote(
            wts.at[index], wts.at[3 - index], ss_g.at[index], rs_w.at[3 - index, 0], mate, p
        )

    def wait_blocks(place):
        def one(k, carry):
            dst = pts.at[place, :, pl.ds(pl.multiple_of(k * 512, 512), 512)]
            remote(pts_in.at[0], dst, ss_u, rs_p.at[place, k], d, p).wait_recv()
            return carry

        lax.fori_loop(0, 4, one, 0)

    def take_pts(n):
        @pl.when(early)
        def _():
            wait_blocks(n)
            pts_pass(n).start()

        @pl.when(jnp.logical_not(early))
        def _():
            place = 5 - n
            remote(pts.at[place], pts.at[place], ss_u, rs_p.at[place, 0], d, p).wait_recv()

    def take_wts(n):
        @pl.when(early)
        def _():
            def one(k, carry):
                dst = wts.at[n - 1, :, pl.ds(pl.multiple_of(k * 512, 512), 512)]
                src = wsrc.at[pl.ds(0, 8), :]
                remote(src, dst, ss_u, rs_w.at[n - 1, k], d, p).wait_recv()
                return carry

            lax.fori_loop(0, 4, one, 0)
            wts_pass(n - 1).start()

        @pl.when(jnp.logical_not(early))
        def _():
            index = 4 - n
            remote(wts.at[index], wts.at[index], ss_u, rs_w.at[index, 0], d, p).wait_recv()

    def send_form(values):
        return jnp.concatenate([values[:, 0:1024], values[:, 1024:2048]], axis=0).astype(BF16)

    def advance(sent, index, sums):
        weight = wts[index]
        live = (weight > 0.0).astype(F32)
        count = jnp.sum(live, axis=1, keepdims=True)
        if sums:
            row = rsum[index]
            each = jnp.concatenate(
                [
                    jnp.sum(sent[0:8].astype(F32) * row[:, 0:1024], axis=1, keepdims=True),
                    jnp.sum(sent[8:16].astype(F32) * row[:, 1024:2048], axis=1, keepdims=True),
                ],
                axis=0,
            )
            scale = count / (each[0:8] + each[8:16])
            scaled = live * scale
        out = []
        for n in range(4):
            at = slice(512 * n, 512 * n + 512)
            low_part = jnp.dot(sent, kern[index, 0:1024, at], preferred_element_type=F32)
            high_part = jnp.dot(sent, kern[index, 1024:2048, at], preferred_element_type=F32)
            got = low_part[0:8] + high_part[8:16]
            out.append(got * (scaled if sums else live)[:, at])
        if not sums:
            scale = count / sum(jnp.sum(part, axis=1, keepdims=True) for part in out)
            out = [part * scale for part in out]
        for n in range(4):
            res[index, :, 512 * n : 512 * n + 512] = out[n]
            out[n] = out[n] * weight[:, 512 * n : 512 * n + 512]
        return jnp.concatenate(
            [jnp.concatenate([out[n], out[n + 2]], axis=0).astype(BF16) for n in range(2)], axis=1
        )

    take_pts(1)
    take_pts(2)

    @pl.when(to_next | to_last)
    def _():
        def give_side(group, carry):
            side_copy(group).start()
            return carry

        lax.fori_loop(0, GROUPS, give_side, 0)

    quick = stage <= 1

    def make_kernel(t, carry):
        index = jnp.where(t == 3, 0, jnp.where(early, t + 1, 3 - t))

        @pl.when((t == 1) | (t == 2))
        def _():
            take_pts(t + 2)

        @pl.when(jnp.logical_not(starts) & (t == 0))
        def _():
            take_wts(1)

        @pl.when(jnp.logical_not(starts) & (t < 3))
        def _():
            take_wts(t + 2)

        @pl.when((t < 3) | jnp.logical_not(starts))
        def _():
            @pl.when(t == 3)
            def _():
                wait_blocks(0)

            fill_side(left, pts[index], 1.0, True)
            fill_side(right, pts[index + 1], 2.0, False)

            def rows(r, inner):
                at = pl.ds(pl.multiple_of(r * ROWS, ROWS), ROWS)
                power = lax.dot_general(
                    left[:, at], right[...], (((0,), (0,)), ((), ())), preferred_element_type=F32
                )
                values = jnp.exp(power).astype(BF16)
                kern[index, at, :] = values
                return inner

            def rows_summed(r, inner):
                at = pl.ds(pl.multiple_of(r * ROWS_SUMMED, ROWS_SUMMED), ROWS_SUMMED)
                power = lax.dot_general(
                    left[:, at], right[...], (((0,), (0,)), ((), ())), preferred_element_type=F32
                )
                values = jnp.exp(power).astype(BF16)
                kern[index, at, :] = values
                live = (wts[index, 0:1, :] > 0.0).astype(F32)
                part = jnp.zeros((ROWS_SUMMED, 128), F32)
                for c in range(16):
                    cut = slice(128 * c, 128 * c + 128)
                    part = part + values[:, cut].astype(F32) * live[:, cut]
                rsum[index, :, at] = jnp.concatenate(
                    [
                        jnp.sum(jnp.transpose(part[128 * c : 128 * c + 128]), axis=0, keepdims=True)
                        for c in range(ROWS_SUMMED // 128)
                    ],
                    axis=1,
                )
                return inner

            @pl.when(quick)
            def _():
                lax.fori_loop(0, 2048 // ROWS, rows, 0)

            @pl.when(jnp.logical_not(quick))
            def _():
                lax.fori_loop(0, 2048 // ROWS_SUMMED, rows_summed, 0)

        @pl.when(starts & (t == 0))
        def _():
            take_wts(1)
            weight = wts[0]
            live = (weight > 0.0).astype(F32)
            res[0] = live
            msg[...] = send_form(live * weight)

        @pl.when(starts & (t < 3))
        def _():
            take_wts(t + 2)
            msg[...] = advance(msg[...], index, False)

        return carry

    lax.fori_loop(0, 4, make_kernel, 0)

    def make_fit():
        fill_side(left, pts[jnp.where(fwd, dl + 1, 4 - dl)], 1.0, True)
        fill_side(right, cells_in[0], 2.0, False)

        def rows(r, inner):
            at = pl.ds(pl.multiple_of(r * ROWS_SUMMED, ROWS_SUMMED), ROWS_SUMMED)
            power = lax.dot_general(
                left[:, at], right[...], (((0,), (0,)), ((), ())), preferred_element_type=F32
            )
            fit[at, :] = jnp.exp(power)
            return inner

        lax.fori_loop(0, 2048 // ROWS_SUMMED, rows, 0)

    next_team = jnp.where(fwd, q + 1, q - 1)
    next_core = jnp.where(fwd == (next_team < TEAMS // 2), 1, 0)
    next_day = 4 * next_team + 2 * (1 - xb) + next_core
    hop = remote(msg, msg, ss_u, rs_u, next_day, p)

    def cross(index):
        return remote(res.at[index], oth.at[3 - index], ss_x.at[index], rs_x.at[3 - index], mate, p)

    @pl.when(jnp.logical_not(early))
    def _():
        make_fit()

    @pl.when(jnp.logical_not(starts))
    def _():
        remote(msg, msg, ss_u, rs_u, d, p).wait_recv()

        @pl.when(quick)
        def _():
            def one(index, carry):
                msg[...] = advance(msg[...], index, False)
                return carry

            lax.fori_loop(0, 4, one, 0)

        @pl.when(jnp.logical_not(quick))
        def _():
            sent = msg[...]
            for index in range(4):
                sent = advance(sent, index, True)
            msg[...] = sent

    @pl.when(stage < TEAMS - 1)
    def _():
        hop.start()

    def mass_copy(index, k):
        return remote(
            mps.at[index], mbuf.at[g], ss_m.at[index, k], rs_m.at[g], day_at(index + 1), k
        )

    def here(index, k):
        return (day_at(index + 1) == d) & (k == p)

    @pl.when(jnp.logical_not(early))
    def _():
        def one(t, carry):
            index = 3 - t
            remote(res.at[index], oth.at[index], ss_u, rs_x.at[index], d, p).wait_recv()
            mps[index] = jnp.sum(res[index] * wts[index] * oth[index], axis=0, keepdims=True)

            def to(k, inner):
                @pl.when(here(index, k))
                def _():
                    pltpu.make_async_copy(mps.at[index], mbuf.at[g], rs_m.at[g]).start()

                @pl.when(jnp.logical_not(here(index, k)))
                def _():
                    mass_copy(index, k).start()

                return inner

            lax.fori_loop(0, 4, to, 0)
            return carry

        lax.fori_loop(0, 4, one, 0)

    @pl.when(early)
    def _():
        def one(index, carry):
            cross(index).start()
            return carry

        lax.fori_loop(0, 4, one, 0)

    way = jnp.where(fwd, 0, 1)
    rows_g = pl.ds(pl.multiple_of(8 * g, 8), 8)

    def out_copy(index, k):
        return remote(
            res.at[index, :, pl.ds(pl.multiple_of(k * 512, 512), 512)],
            fb_out.at[way, rows_g, :],
            ss_o.at[index, k],
            rs_o.at[way, g],
            day_at(index + 1),
            k,
        )

    def out_days(index, carry):
        def to(k, inner):
            @pl.when(here(index, k))
            def _():
                pltpu.make_async_copy(
                    res.at[index, :, pl.ds(pl.multiple_of(k * 512, 512), 512)],
                    fb_out.at[way, rows_g, :],
                    rs_o.at[way, g],
                ).start()

            @pl.when(jnp.logical_not(here(index, k)))
            def _():
                out_copy(index, k).start()

            return inner

        lax.fori_loop(0, 4, to, 0)
        return carry

    lax.fori_loop(0, 4, out_days, 0)

    @pl.when(early)
    def _():
        make_fit()

    def wait_mass(k, carry):
        remote(mps.at[0], mbuf.at[k], ss_u, rs_m.at[k], d, p).wait_recv()
        return carry

    lax.fori_loop(0, GROUPS, wait_mass, 0)
    mass = mbuf[0]
    for k in range(1, GROUPS):
        mass = mass + mbuf[k]
    mass_total = jnp.sum(mass, axis=1, keepdims=True)
    mrow[...] = jnp.zeros_like(mrow)
    for k in range(16):
        mrow[k : k + 1, :] = mass[:, 128 * k : 128 * k + 128]
    columns = jnp.transpose(mrow[...])
    total = jnp.zeros((8, 2048), F32)
    for k in range(16):
        block = fit[128 * k : 128 * k + 128, :] * columns[:, k : k + 1]
        total = total + jnp.sum(block.reshape(16, 8, 2048), axis=0)
    density = jnp.sum(total, axis=0, keepdims=True) / mass_total
    cell = lax.broadcasted_iota(jnp.int32, (1, 2048), 1) + p * 2048
    inverse = (cell < cc_in[0]).astype(F32) / density
    for k in range(16):
        part = jnp.zeros((128, 128), F32)
        for c in range(16):
            part = part + (
                fit[128 * k : 128 * k + 128, 128 * c : 128 * c + 128]
                * inverse[:, 128 * c : 128 * c + 128]
            )
        rpart[k // 4, :, 128 * (k % 4) : 128 * (k % 4) + 128] = jnp.sum(
            jnp.transpose(part), axis=0, keepdims=True
        )

    def ratio_copy(k):
        return remote(rpart.at[k], rbuf.at[p], ss_r.at[k], rs_r.at[p], d, k)

    def ratio_to(k, carry):
        @pl.when(k == p)
        def _():
            pltpu.make_async_copy(rpart.at[k], rbuf.at[p], rs_r.at[p]).start()

        @pl.when(k != p)
        def _():
            ratio_copy(k).start()

        return carry

    lax.fori_loop(0, 4, ratio_to, 0)

    def ratio_wait(k, carry):
        remote(rpart.at[0], rbuf.at[k], ss_u, rs_r.at[k], d, p).wait_recv()
        return carry

    lax.fori_loop(0, 4, ratio_wait, 0)
    summed = rbuf[0] + rbuf[1] + rbuf[2] + rbuf[3]
    fit_out[...] = live_own / jnp.full((1, 512), cc_in[0], jnp.int32).astype(F32) * summed

    def close_give(group, carry):
        @pl.when(jnp.logical_not(is_self(group)))
        def _():
            pts_copy(group, q, 1, place_own, ss_p.at[group]).wait_send()
            wts_copy(group).wait_send()

        @pl.when(to_next | to_last)
        def _():
            side_copy(group).wait_send()

        def arrived(way_in, inner):
            remote(
                res.at[0, :, pl.ds(0, 512)],
                fb_out.at[way_in, pl.ds(pl.multiple_of(8 * group, 8), 8), :],
                ss_u,
                rs_o.at[way_in, group],
                d,
                p,
            ).wait_recv()
            return inner

        lax.fori_loop(0, 2, arrived, 0)
        return carry

    lax.fori_loop(0, GROUPS, close_give, 0)

    def close_four(index, carry):
        @pl.when(early)
        def _():
            pts_pass(index + 1).wait_send()
            wts_pass(index).wait_send()
            cross(index).wait_send()

        @pl.when(index != p)
        def _():
            ratio_copy(index).wait_send()

        def to(k, inner):
            @pl.when(jnp.logical_not(here(index, k)))
            def _():
                out_copy(index, k).wait_send()

                @pl.when(jnp.logical_not(early))
                def _():
                    mass_copy(index, k).wait_send()

            return inner

        lax.fori_loop(0, 4, to, 0)
        return carry

    lax.fori_loop(0, 4, close_four, 0)

    @pl.when(stage < TEAMS - 1)
    def _():
        hop.wait_send()


def shards(points, cells, clone_weight, potential, support_count, cell_count):
    vmem = pl.BlockSpec(memory_space=pltpu.VMEM)
    smem = pl.BlockSpec(memory_space=pltpu.SMEM)
    dma = pltpu.SemaphoreType.DMA
    both, ratio = pl.pallas_call(
        body,
        out_shape=(
            jax.ShapeDtypeStruct((2, 64, 512), F32),
            jax.ShapeDtypeStruct((1, 512), F32),
        ),
        in_specs=[vmem, vmem, vmem, vmem, smem, smem],
        out_specs=(pl.BlockSpec(memory_space=pl.ANY), vmem),
        scratch_shapes=[
            pltpu.VMEM((4, 2048, 2048), BF16),
            pltpu.VMEM((4, 1, 2048), F32),
            pltpu.VMEM((2048, 2048), F32),
            pltpu.VMEM((5, 64, 2048), BF16),
            pltpu.VMEM((4, 8, 2048), F32),
            pltpu.VMEM((4, 8, 2048), F32),
            pltpu.VMEM((4, 8, 2048), F32),
            pltpu.VMEM((16, 1024), BF16),
            pltpu.VMEM((64, 512), F32),
            pltpu.VMEM((DEPTH, 2048), BF16),
            pltpu.VMEM((DEPTH, 2048), BF16),
            pltpu.VMEM((4, 1, 2048), F32),
            pltpu.VMEM((GROUPS, 1, 2048), F32),
            pltpu.VMEM((128, 128), F32),
            pltpu.VMEM((4, 1, 512), F32),
            pltpu.VMEM((4, 1, 512), F32),
            dma((5, 4)),
            dma((4, 4)),
            dma((GROUPS,)),
            dma((GROUPS,)),
            dma((GROUPS,)),
            dma((4,)),
            dma((4,)),
            dma,
            dma,
            dma((2, GROUPS)),
            dma((4, 4)),
            dma((4,)),
            dma((4,)),
            dma((GROUPS,)),
            dma((4, 4)),
            dma((4,)),
            dma((4,)),
        ],
        compiler_params=pltpu.CompilerParams(
            collective_id=0, has_side_effects=True, vmem_limit_bytes=62 * 1024 * 1024
        ),
        name="days",
    )(points, cells, clone_weight, potential, support_count, cell_count)
    return both[0][None], both[1][None], ratio


def solution(mesh):
    in_specs = (
        P("day", None, "pt"),
        P("day", None, "pt"),
        P("day", None, "pt"),
        P("day", "pt"),
        P("day"),
        P("day"),
    )
    out_specs = (P("day", None, "pt"), P("day", None, "pt"), P("day", "pt"))
    return jax.shard_map(shards, mesh=mesh, in_specs=in_specs, out_specs=out_specs, check_vma=False)
```

```python
import jax
import jax.numpy as jnp
from jax import lax
from jax.experimental import pallas as pl
from jax.experimental.pallas import tpu as pltpu
from jax.sharding import PartitionSpec as P

MESH = pl.DeviceIdType.MESH
F32 = jnp.float32
BF16 = jnp.bfloat16
TEAMS = 8
GROUPS = 8
DEPTH = 80
ROWS = 2048
PART = 512
ROWS_SUMMED = 512


def remote(src, dst, send_sem, recv_sem, day, pt):
    return pltpu.make_async_remote_copy(
        src_ref=src,
        dst_ref=dst,
        send_sem=send_sem,
        recv_sem=recv_sem,
        device_id=(day, pt),
        device_id_type=MESH,
    )


def parts_of(norm):
    first = norm.astype(BF16).astype(F32)
    rest = norm - first
    second = rest.astype(BF16).astype(F32)
    third = (rest - second).astype(BF16).astype(F32)
    return first, second, third


def fill_side(side, coords, factor, norms_first):
    wide = coords.astype(F32)
    norm = -jnp.sum(wide * wide, axis=0, keepdims=True)
    one, two, three = parts_of(norm)
    shape = (DEPTH - 64, coords.shape[1])
    row = lax.broadcasted_iota(jnp.int32, shape, 0)
    if not norms_first:
        row = jnp.where(row < 3, row + 3, jnp.where(row < 6, row - 3, row))
    extra = jnp.where(row == 0, one, jnp.where(row == 1, two, jnp.where(row == 2, three, 0.0)))
    extra = jnp.where((row >= 3) & (row < 6), 1.0, extra)
    side[0:64, :] = (wide * factor).astype(BF16)
    side[64:DEPTH, :] = extra.astype(BF16)


def body(
    pts_in, cells_in, cw_in, pot_in, sc_in, cc_in, fb_out, fit_out,
    kern, rsum, fit, pts, wts, res, oth, msg, alt, turn, wsrc, left, right, mps, mbuf, mrow, rpart, rbuf,
    rs_p, rs_w, ss_p, ss_w, ss_i, ss_f, ss_g, rs_u, ss_u, rs_o, ss_o, rs_x, ss_x, rs_m, ss_m,
    rs_r, ss_r, rs_h, ss_h, rs_k, ss_k,
):
    d = lax.axis_index("day")
    p = lax.axis_index("pt")
    q = d // 4
    dl = d % 4
    core = d % 2
    pair = q % 2
    xb = (d // 2) % 2
    bit = jnp.where(pair == 0, xb, 1 - xb)
    g = 2 * p + bit
    early = core == 1
    low = q < TEAMS // 2
    fwd = early == low
    stage = jnp.where(fwd, q, TEAMS - 1 - q)
    starts = stage == 0
    own_col = pl.multiple_of(p * 512, 512)

    def day_at(place):
        return 4 * q + jnp.where(fwd, place - 1, 4 - place)

    def chain_day(team, group, at_core):
        flip = team % 2
        side = group % 2
        return 4 * team + 2 * jnp.where(flip == 0, side, 1 - side) + at_core

    barrier = pltpu.get_barrier_semaphore()

    def greet(n, carry):
        day = 4 * q + n // 4
        pt = n % 4

        @pl.when(jnp.logical_not((day == d) & (pt == p)))
        def _():
            pl.semaphore_signal(barrier, inc=1, device_id=(day, pt), device_id_type=MESH)

        return carry

    lax.fori_loop(0, 16, greet, 0)

    @pl.when(jnp.logical_not(starts))
    def _():
        last_team = jnp.where(fwd, q - 1, q + 1)
        last_core = jnp.where(fwd == (last_team < TEAMS // 2), 1, 0)
        last_day = 4 * last_team + 2 * (1 - xb) + last_core
        pl.semaphore_signal(barrier, inc=1, device_id=(last_day, p), device_id_type=MESH)

        def greet_side(pt, carry):
            day = jnp.where(fwd, 4 * q - 1, 4 * q + 4)
            pl.semaphore_signal(barrier, inc=1, device_id=(day, pt), device_id_type=MESH)
            return carry

        lax.fori_loop(0, 4, greet_side, 0)

    slot_own = lax.broadcasted_iota(jnp.int32, (1, 512), 1) + p * 512
    live_own = (slot_own < sc_in[0]).astype(F32)
    wsrc[...] = cw_in[0] * (pot_in[...] * live_own)

    to_next = (dl == 3) & (q < TEAMS - 1)
    to_last = (dl == 0) & (q > 0)
    others = 15 + jnp.where(to_next | to_last, GROUPS, 0) + jnp.where(stage < TEAMS - 1, 1, 0)
    pl.semaphore_wait(barrier, others)

    place_own = jnp.where(low, dl + 1, 4 - dl)

    def pts_copy(group, team, at_core, place, send_sem):
        return remote(
            pts_in.at[0],
            pts.at[place, :, pl.ds(own_col, 512)],
            send_sem,
            rs_p.at[place, p],
            chain_day(team, group, at_core),
            group // 2,
        )

    def wts_copy(group):
        return remote(
            wsrc.at[pl.ds(pl.multiple_of(8 * group, 8), 8), :],
            wts.at[place_own - 1, :, pl.ds(own_col, 512)],
            ss_w.at[group],
            rs_w.at[place_own - 1, p],
            chain_day(q, group, 1),
            group // 2,
        )

    def is_self(group):
        return (chain_day(q, group, 1) == d) & (group // 2 == p)

    def give_pts(group, carry):
        @pl.when(is_self(group))
        def _():
            pltpu.make_async_copy(
                pts_in.at[0], pts.at[place_own, :, pl.ds(own_col, 512)], rs_p.at[place_own, p]
            ).start()

        @pl.when(jnp.logical_not(is_self(group)))
        def _():
            pts_copy(group, q, 1, place_own, ss_p.at[group]).start()

        return carry

    def give_wts(group, carry):
        @pl.when(is_self(group))
        def _():
            pltpu.make_async_copy(
                wsrc.at[pl.ds(pl.multiple_of(8 * group, 8), 8), :],
                wts.at[place_own - 1, :, pl.ds(own_col, 512)],
                rs_w.at[place_own - 1, p],
            ).start()

        @pl.when(jnp.logical_not(is_self(group)))
        def _():
            wts_copy(group).start()

        return carry

    def give():
        def turned(group):
            return lax.rem(group + 2 * p + 2, GROUPS)

        lax.fori_loop(0, GROUPS, lambda n, carry: give_pts(turned(n), carry), 0)
        lax.fori_loop(0, GROUPS, lambda n, carry: give_wts(turned(n), carry), 0)

    give()

    side_team = jnp.where(dl == 3, q + 1, q - 1)
    side_core = jnp.where(
        dl == 3,
        jnp.where(side_team < TEAMS // 2, 1, 0),
        jnp.where(side_team < TEAMS // 2, 0, 1),
    )

    def side_copy(group):
        return pts_copy(group, side_team, side_core, 0, ss_i.at[group])

    mate = d - 1

    def pts_pass(place):
        return remote(
            pts.at[place], pts.at[5 - place], ss_f.at[place - 1], rs_p.at[5 - place, 0], mate, p
        )

    def wts_pass(index):
        return remote(
            wts.at[index], wts.at[3 - index], ss_g.at[index], rs_w.at[3 - index, 0], mate, p
        )

    def wait_blocks(place):
        def one(k, carry):
            dst = pts.at[place, :, pl.ds(pl.multiple_of(k * 512, 512), 512)]
            remote(pts_in.at[0], dst, ss_u, rs_p.at[place, k], d, p).wait_recv()
            return carry

        lax.fori_loop(0, 4, one, 0)

    def take_pts(n):
        @pl.when(early)
        def _():
            wait_blocks(n)
            pts_pass(n).start()

        @pl.when(jnp.logical_not(early))
        def _():
            place = 5 - n
            remote(pts.at[place], pts.at[place], ss_u, rs_p.at[place, 0], d, p).wait_recv()

    def take_wts(n):
        @pl.when(early)
        def _():
            def one(k, carry):
                dst = wts.at[n - 1, :, pl.ds(pl.multiple_of(k * 512, 512), 512)]
                src = wsrc.at[pl.ds(0, 8), :]
                remote(src, dst, ss_u, rs_w.at[n - 1, k], d, p).wait_recv()
                return carry

            lax.fori_loop(0, 4, one, 0)
            wts_pass(n - 1).start()

        @pl.when(jnp.logical_not(early))
        def _():
            index = 4 - n
            remote(wts.at[index], wts.at[index], ss_u, rs_w.at[index, 0], d, p).wait_recv()

    def send_form(values):
        return jnp.concatenate([values[:, 0:1024], values[:, 1024:2048]], axis=0).astype(BF16)

    def advance(sent, index, sums, place=None):
        place = index if place is None else place
        weight = wts[place]
        live = (weight > 0.0).astype(F32)
        count = jnp.sum(live, axis=1, keepdims=True)
        if sums:
            row = rsum[index]
            each = jnp.concatenate(
                [
                    jnp.sum(sent[0:8].astype(F32) * row[:, 0:1024], axis=1, keepdims=True),
                    jnp.sum(sent[8:16].astype(F32) * row[:, 1024:2048], axis=1, keepdims=True),
                ],
                axis=0,
            )
            scale = count / (each[0:8] + each[8:16])
            scaled = live * scale
        out = []
        for n in range(4):
            at = slice(512 * n, 512 * n + 512)
            low_part = jnp.dot(sent, kern[index, 0:1024, at], preferred_element_type=F32)
            high_part = jnp.dot(sent, kern[index, 1024:2048, at], preferred_element_type=F32)
            got = low_part[0:8] + high_part[8:16]
            out.append(got * (scaled if sums else live)[:, at])
        if not sums:
            scale = count / sum(jnp.sum(part, axis=1, keepdims=True) for part in out)
            out = [part * scale for part in out]
        for n in range(4):
            res[place, :, 512 * n : 512 * n + 512] = out[n]
            out[n] = out[n] * weight[:, 512 * n : 512 * n + 512]
        return jnp.concatenate(
            [jnp.concatenate([out[n], out[n + 2]], axis=0).astype(BF16) for n in range(2)], axis=1
        )

    take_pts(1)
    take_pts(2)

    @pl.when(to_next | to_last)
    def _():
        def give_side(group, carry):
            side_copy(group).start()
            return carry

        lax.fori_loop(0, GROUPS, give_side, 0)

    quick = stage <= 1
    helps = stage == TEAMS - 1
    ask = remote(msg, alt, ss_h, rs_h, mate, p)
    reply = remote(turn, alt, ss_h, rs_h, d + 1, p)
    reply_res = remote(res.at[1], res.at[2], ss_k, rs_k, d + 1, p)

    def make_kernel(t, carry):
        index = jnp.where((t == 3) | (t < 0), 0, jnp.where(early, t + 1, 3 - t))

        first = t < 0
        paired = starts | helps

        @pl.when(((t == 1) & jnp.logical_not(paired)) | (t == 2))
        def _():
            take_pts(t + 2)

        @pl.when(jnp.logical_not(paired) & (t == 0))
        def _():
            take_wts(1)

        @pl.when((jnp.logical_not(paired) & (t < 3)) | (helps & (t == 2)))
        def _():
            take_wts(t + 2)

        @pl.when(first)
        def _():
            take_pts(3)
            for n in range(1, 4):
                take_wts(n)

        @pl.when(jnp.logical_not(starts) | (t == 0) | (t == 2))
        def _():
            @pl.when(t == 3)
            def _():
                wait_blocks(0)

            fill_side(left, pts[jnp.where(first, 3, index)], 1.0, True)
            fill_side(right, pts[jnp.where(first, 2, index + 1)], 2.0, False)

            def rows(r, inner):
                for c in range(ROWS // PART):
                    at = pl.ds(pl.multiple_of(r * ROWS + PART * c, PART), PART)
                    power = lax.dot_general(
                        left[:, at],
                        right[...],
                        (((0,), (0,)), ((), ())),
                        preferred_element_type=F32,
                    )
                    kern[index, at, :] = jnp.exp(power).astype(BF16)
                return inner

            def rows_summed(r, inner):
                at = pl.ds(pl.multiple_of(r * ROWS_SUMMED, ROWS_SUMMED), ROWS_SUMMED)
                power = lax.dot_general(
                    left[:, at], right[...], (((0,), (0,)), ((), ())), preferred_element_type=F32
                )
                values = jnp.exp(power).astype(BF16)
                kern[index, at, :] = values
                live = (wts[index, 0:1, :] > 0.0).astype(F32)
                part = jnp.zeros((ROWS_SUMMED, 128), F32)
                for c in range(16):
                    cut = slice(128 * c, 128 * c + 128)
                    part = part + values[:, cut].astype(F32) * live[:, cut]
                rsum[index, :, at] = jnp.concatenate(
                    [
                        jnp.sum(jnp.transpose(part[128 * c : 128 * c + 128]), axis=0, keepdims=True)
                        for c in range(ROWS_SUMMED // 128)
                    ],
                    axis=1,
                )
                return inner

            @pl.when(quick | first)
            def _():
                lax.fori_loop(0, 2048 // ROWS, rows, 0)

            @pl.when(jnp.logical_not(quick | first))
            def _():
                lax.fori_loop(0, 2048 // ROWS_SUMMED, rows_summed, 0)

        @pl.when(starts & (t == 0))
        def _():
            take_pts(3)
            for n in range(1, 4):
                take_wts(n)
            weight = wts[0]
            live = (weight > 0.0).astype(F32)
            res[0] = live
            msg[...] = send_form(live * weight)

        @pl.when(starts & (t == 2))
        def _():
            take_wts(4)
            ask.wait_send()
            ask.wait_recv()
            reply_res.wait_recv()
            msg[...] = alt[...]

        @pl.when(first)
        def _():
            ask.wait_recv()
            turn[...] = alt[...]

        @pl.when((starts & ((t == 0) | (t == 2))) | first)
        def _():
            @pl.when(first)
            def _():
                turn[...] = advance(turn[...], 0, False, 1)
                reply.start()
                reply_res.start()
                reply.wait_send()
                reply_res.wait_send()

            @pl.when(starts)
            def _():
                msg[...] = advance(msg[...], index, False)

            @pl.when(starts & (t == 0))
            def _():
                ask.start()

        return carry

    lax.fori_loop(jnp.where(helps, -1, 0), 4, make_kernel, 0)

    def make_fit():
        fill_side(left, pts[jnp.where(fwd, dl + 1, 4 - dl)], 1.0, True)
        fill_side(right, cells_in[0], 2.0, False)

        def rows(r, inner):
            at = pl.ds(pl.multiple_of(r * ROWS_SUMMED, ROWS_SUMMED), ROWS_SUMMED)
            power = lax.dot_general(
                left[:, at], right[...], (((0,), (0,)), ((), ())), preferred_element_type=F32
            )
            fit[at, :] = jnp.exp(power)
            return inner

        lax.fori_loop(0, 2048 // ROWS_SUMMED, rows, 0)

    next_team = jnp.where(fwd, q + 1, q - 1)
    next_core = jnp.where(fwd == (next_team < TEAMS // 2), 1, 0)
    next_day = 4 * next_team + 2 * (1 - xb) + next_core
    hop = remote(msg, msg, ss_u, rs_u, next_day, p)

    def cross(index):
        return remote(res.at[index], oth.at[3 - index], ss_x.at[index], rs_x.at[3 - index], mate, p)

    @pl.when(jnp.logical_not(early))
    def _():
        make_fit()

    @pl.when(jnp.logical_not(starts))
    def _():
        remote(msg, msg, ss_u, rs_u, d, p).wait_recv()

        @pl.when(quick)
        def _():
            def one(index, carry):
                msg[...] = advance(msg[...], index, False)
                return carry

            lax.fori_loop(0, 4, one, 0)

        @pl.when(jnp.logical_not(quick))
        def _():
            sent = msg[...]
            for index in range(4):
                sent = advance(sent, index, True)
            msg[...] = sent

    @pl.when(stage < TEAMS - 1)
    def _():
        hop.start()

    def mass_copy(index, k):
        return remote(
            mps.at[index], mbuf.at[g], ss_m.at[index, k], rs_m.at[g], day_at(index + 1), k
        )

    def here(index, k):
        return (day_at(index + 1) == d) & (k == p)

    @pl.when(jnp.logical_not(early))
    def _():
        def one(t, carry):
            index = 3 - t
            remote(res.at[index], oth.at[index], ss_u, rs_x.at[index], d, p).wait_recv()
            mps[index] = jnp.sum(res[index] * wts[index] * oth[index], axis=0, keepdims=True)

            def to(k, inner):
                @pl.when(here(index, k))
                def _():
                    pltpu.make_async_copy(mps.at[index], mbuf.at[g], rs_m.at[g]).start()

                @pl.when(jnp.logical_not(here(index, k)))
                def _():
                    mass_copy(index, k).start()

                return inner

            lax.fori_loop(0, 4, to, 0)
            return carry

        lax.fori_loop(0, 4, one, 0)

    @pl.when(early)
    def _():
        def one(index, carry):
            cross(index).start()
            return carry

        lax.fori_loop(0, 4, one, 0)

    way = jnp.where(fwd, 0, 1)
    rows_g = pl.ds(pl.multiple_of(8 * g, 8), 8)

    def out_copy(index, k):
        return remote(
            res.at[index, :, pl.ds(pl.multiple_of(k * 512, 512), 512)],
            fb_out.at[way, rows_g, :],
            ss_o.at[index, k],
            rs_o.at[way, g],
            day_at(index + 1),
            k,
        )

    def out_days(index, carry):
        def to(k, inner):
            @pl.when(here(index, k))
            def _():
                pltpu.make_async_copy(
                    res.at[index, :, pl.ds(pl.multiple_of(k * 512, 512), 512)],
                    fb_out.at[way, rows_g, :],
                    rs_o.at[way, g],
                ).start()

            @pl.when(jnp.logical_not(here(index, k)))
            def _():
                out_copy(index, k).start()

            return inner

        lax.fori_loop(0, 4, to, 0)
        return carry

    lax.fori_loop(0, 4, out_days, 0)

    @pl.when(early)
    def _():
        make_fit()

    def wait_mass(k, carry):
        remote(mps.at[0], mbuf.at[k], ss_u, rs_m.at[k], d, p).wait_recv()
        return carry

    lax.fori_loop(0, GROUPS, wait_mass, 0)
    mass = mbuf[0]
    for k in range(1, GROUPS):
        mass = mass + mbuf[k]
    mass_total = jnp.sum(mass, axis=1, keepdims=True)
    mrow[...] = jnp.zeros_like(mrow)
    for k in range(16):
        mrow[k : k + 1, :] = mass[:, 128 * k : 128 * k + 128]
    columns = jnp.transpose(mrow[...])
    total = jnp.zeros((8, 2048), F32)
    for k in range(16):
        block = fit[128 * k : 128 * k + 128, :] * columns[:, k : k + 1]
        total = total + jnp.sum(block.reshape(16, 8, 2048), axis=0)
    density = jnp.sum(total, axis=0, keepdims=True) / mass_total
    cell = lax.broadcasted_iota(jnp.int32, (1, 2048), 1) + p * 2048
    inverse = (cell < cc_in[0]).astype(F32) / density
    for k in range(16):
        part = jnp.zeros((128, 128), F32)
        for c in range(16):
            part = part + (
                fit[128 * k : 128 * k + 128, 128 * c : 128 * c + 128]
                * inverse[:, 128 * c : 128 * c + 128]
            )
        rpart[k // 4, :, 128 * (k % 4) : 128 * (k % 4) + 128] = jnp.sum(
            jnp.transpose(part), axis=0, keepdims=True
        )

    def ratio_copy(k):
        return remote(rpart.at[k], rbuf.at[p], ss_r.at[k], rs_r.at[p], d, k)

    def ratio_to(k, carry):
        @pl.when(k == p)
        def _():
            pltpu.make_async_copy(rpart.at[k], rbuf.at[p], rs_r.at[p]).start()

        @pl.when(k != p)
        def _():
            ratio_copy(k).start()

        return carry

    lax.fori_loop(0, 4, ratio_to, 0)

    def close_give(group, carry):
        @pl.when(jnp.logical_not(is_self(group)))
        def _():
            pts_copy(group, q, 1, place_own, ss_p.at[group]).wait_send()
            wts_copy(group).wait_send()

        @pl.when(to_next | to_last)
        def _():
            side_copy(group).wait_send()

        def arrived(way_in, inner):
            remote(
                res.at[0, :, pl.ds(0, 512)],
                fb_out.at[way_in, pl.ds(pl.multiple_of(8 * group, 8), 8), :],
                ss_u,
                rs_o.at[way_in, group],
                d,
                p,
            ).wait_recv()
            return inner

        lax.fori_loop(0, 2, arrived, 0)
        return carry

    lax.fori_loop(0, GROUPS, close_give, 0)

    def close_four(index, carry):
        @pl.when(early)
        def _():
            pts_pass(index + 1).wait_send()
            wts_pass(index).wait_send()
            cross(index).wait_send()

        def to(k, inner):
            @pl.when(jnp.logical_not(here(index, k)))
            def _():
                out_copy(index, k).wait_send()

                @pl.when(jnp.logical_not(early))
                def _():
                    mass_copy(index, k).wait_send()

            return inner

        lax.fori_loop(0, 4, to, 0)
        return carry

    lax.fori_loop(0, 4, close_four, 0)

    @pl.when(stage < TEAMS - 1)
    def _():
        hop.wait_send()

    def ratio_wait(k, carry):
        remote(rpart.at[0], rbuf.at[k], ss_u, rs_r.at[k], d, p).wait_recv()
        return carry

    lax.fori_loop(0, 4, ratio_wait, 0)
    summed = rbuf[0] + rbuf[1] + rbuf[2] + rbuf[3]
    fit_out[...] = live_own / jnp.full((1, 512), cc_in[0], jnp.int32).astype(F32) * summed

    def close_ratio(k, carry):
        @pl.when(k != p)
        def _():
            ratio_copy(k).wait_send()

        return carry

    lax.fori_loop(0, 4, close_ratio, 0)


def shards(points, cells, clone_weight, potential, support_count, cell_count):
    vmem = pl.BlockSpec(memory_space=pltpu.VMEM)
    smem = pl.BlockSpec(memory_space=pltpu.SMEM)
    dma = pltpu.SemaphoreType.DMA
    both, ratio = pl.pallas_call(
        body,
        out_shape=(
            jax.ShapeDtypeStruct((2, 64, 512), F32),
            jax.ShapeDtypeStruct((1, 512), F32),
        ),
        in_specs=[vmem, vmem, vmem, vmem, smem, smem],
        out_specs=(pl.BlockSpec(memory_space=pl.ANY), vmem),
        scratch_shapes=[
            pltpu.VMEM((4, 2048, 2048), BF16),
            pltpu.VMEM((4, 1, 2048), F32),
            pltpu.VMEM((2048, 2048), F32),
            pltpu.VMEM((5, 64, 2048), BF16),
            pltpu.VMEM((4, 8, 2048), F32),
            pltpu.VMEM((4, 8, 2048), F32),
            pltpu.VMEM((4, 8, 2048), F32),
            pltpu.VMEM((16, 1024), BF16),
            pltpu.VMEM((16, 1024), BF16),
            pltpu.VMEM((16, 1024), BF16),
            pltpu.VMEM((64, 512), F32),
            pltpu.VMEM((DEPTH, 2048), BF16),
            pltpu.VMEM((DEPTH, 2048), BF16),
            pltpu.VMEM((4, 1, 2048), F32),
            pltpu.VMEM((GROUPS, 1, 2048), F32),
            pltpu.VMEM((128, 128), F32),
            pltpu.VMEM((4, 1, 512), F32),
            pltpu.VMEM((4, 1, 512), F32),
            dma((5, 4)),
            dma((4, 4)),
            dma((GROUPS,)),
            dma((GROUPS,)),
            dma((GROUPS,)),
            dma((4,)),
            dma((4,)),
            dma,
            dma,
            dma((2, GROUPS)),
            dma((4, 4)),
            dma((4,)),
            dma((4,)),
            dma((GROUPS,)),
            dma((4, 4)),
            dma((4,)),
            dma((4,)),
            dma,
            dma,
            dma,
            dma,
        ],
        compiler_params=pltpu.CompilerParams(
            collective_id=0, has_side_effects=True, vmem_limit_bytes=62 * 1024 * 1024
        ),
        name="days",
    )(points, cells, clone_weight, potential, support_count, cell_count)
    return both[0][None], both[1][None], ratio


def solution(mesh):
    in_specs = (
        P("day", None, "pt"),
        P("day", None, "pt"),
        P("day", None, "pt"),
        P("day", "pt"),
        P("day"),
        P("day"),
    )
    out_specs = (P("day", None, "pt"), P("day", None, "pt"), P("day", "pt"))
    return jax.shard_map(shards, mesh=mesh, in_specs=in_specs, out_specs=out_specs, check_vma=False)
```

```python
import jax
import jax.numpy as jnp
from jax import lax
from jax.experimental import pallas as pl
from jax.experimental.pallas import tpu as pltpu
from jax.sharding import PartitionSpec as P

MESH = pl.DeviceIdType.MESH
F32 = jnp.float32
BF16 = jnp.bfloat16
TEAMS = 8
GROUPS = 8
DEPTH = 80
ROWS = 2048
PART = 512
ROWS_SUMMED = 512


def remote(src, dst, send_sem, recv_sem, day, pt):
    return pltpu.make_async_remote_copy(
        src_ref=src,
        dst_ref=dst,
        send_sem=send_sem,
        recv_sem=recv_sem,
        device_id=(day, pt),
        device_id_type=MESH,
    )


def parts_of(norm):
    first = norm.astype(BF16).astype(F32)
    rest = norm - first
    second = rest.astype(BF16).astype(F32)
    third = (rest - second).astype(BF16).astype(F32)
    return first, second, third


def fill_side(side, coords, factor, norms_first):
    wide = coords.astype(F32)
    norm = -jnp.sum(wide * wide, axis=0, keepdims=True)
    one, two, three = parts_of(norm)
    shape = (DEPTH - 64, coords.shape[1])
    row = lax.broadcasted_iota(jnp.int32, shape, 0)
    if not norms_first:
        row = jnp.where(row < 3, row + 3, jnp.where(row < 6, row - 3, row))
    extra = jnp.where(row == 0, one, jnp.where(row == 1, two, jnp.where(row == 2, three, 0.0)))
    extra = jnp.where((row >= 3) & (row < 6), 1.0, extra)
    side[0:64, :] = (wide * factor).astype(BF16)
    side[64:DEPTH, :] = extra.astype(BF16)


def body(
    pts_in, cells_in, cw_in, pot_in, sc_in, cc_in, fb_out, fit_out,
    kern, rsum, fit, pts, wts, res, oth, msg, alt, turn, wsrc, left, right, mps, mbuf, mrow, rpart, rbuf,
    rs_p, rs_w, ss_p, ss_w, ss_i, ss_f, ss_g, rs_u, ss_u, rs_o, ss_o, rs_x, ss_x, rs_m, ss_m,
    rs_r, ss_r, rs_h, ss_h, rs_k, ss_k,
):
    d = lax.axis_index("day")
    p = lax.axis_index("pt")
    q = d // 4
    dl = d % 4
    core = d % 2
    pair = q % 2
    xb = (d // 2) % 2
    bit = jnp.where(pair == 0, xb, 1 - xb)
    g = 2 * p + bit
    early = core == 1
    low = q < TEAMS // 2
    fwd = early == low
    stage = jnp.where(fwd, q, TEAMS - 1 - q)
    starts = stage == 0
    own_col = pl.multiple_of(p * 512, 512)

    def day_at(place):
        return 4 * q + jnp.where(fwd, place - 1, 4 - place)

    def chain_day(team, group, at_core):
        flip = team % 2
        side = group % 2
        return 4 * team + 2 * jnp.where(flip == 0, side, 1 - side) + at_core

    barrier = pltpu.get_barrier_semaphore()

    def greet(n, carry):
        day = 4 * q + n // 4
        pt = n % 4

        @pl.when(jnp.logical_not((day == d) & (pt == p)))
        def _():
            pl.semaphore_signal(barrier, inc=1, device_id=(day, pt), device_id_type=MESH)

        return carry

    lax.fori_loop(0, 16, greet, 0)

    @pl.when(jnp.logical_not(starts))
    def _():
        last_team = jnp.where(fwd, q - 1, q + 1)
        last_core = jnp.where(fwd == (last_team < TEAMS // 2), 1, 0)
        last_day = 4 * last_team + 2 * (1 - xb) + last_core
        pl.semaphore_signal(barrier, inc=1, device_id=(last_day, p), device_id_type=MESH)

        def greet_side(pt, carry):
            day = jnp.where(fwd, 4 * q - 1, 4 * q + 4)
            pl.semaphore_signal(barrier, inc=1, device_id=(day, pt), device_id_type=MESH)
            return carry

        lax.fori_loop(0, 4, greet_side, 0)

    slot_own = lax.broadcasted_iota(jnp.int32, (1, 512), 1) + p * 512
    live_own = (slot_own < sc_in[0]).astype(F32)
    wsrc[...] = cw_in[0] * (pot_in[...] * live_own)

    to_next = (dl == 3) & (q < TEAMS - 1)
    to_last = (dl == 0) & (q > 0)
    others = 15 + jnp.where(to_next | to_last, GROUPS, 0) + jnp.where(stage < TEAMS - 1, 1, 0)
    pl.semaphore_wait(barrier, others)

    place_own = jnp.where(low, dl + 1, 4 - dl)

    def pts_copy(group, team, at_core, place, send_sem):
        return remote(
            pts_in.at[0],
            pts.at[place, :, pl.ds(own_col, 512)],
            send_sem,
            rs_p.at[place, p],
            chain_day(team, group, at_core),
            group // 2,
        )

    def wts_copy(group):
        return remote(
            wsrc.at[pl.ds(pl.multiple_of(8 * group, 8), 8), :],
            wts.at[place_own - 1, :, pl.ds(own_col, 512)],
            ss_w.at[group],
            rs_w.at[place_own - 1, p],
            chain_day(q, group, 1),
            group // 2,
        )

    def is_self(group):
        return (chain_day(q, group, 1) == d) & (group // 2 == p)

    def give_pts(group, carry):
        @pl.when(is_self(group))
        def _():
            pltpu.make_async_copy(
                pts_in.at[0], pts.at[place_own, :, pl.ds(own_col, 512)], rs_p.at[place_own, p]
            ).start()

        @pl.when(jnp.logical_not(is_self(group)))
        def _():
            pts_copy(group, q, 1, place_own, ss_p.at[group]).start()

        return carry

    def give_wts(group, carry):
        @pl.when(is_self(group))
        def _():
            pltpu.make_async_copy(
                wsrc.at[pl.ds(pl.multiple_of(8 * group, 8), 8), :],
                wts.at[place_own - 1, :, pl.ds(own_col, 512)],
                rs_w.at[place_own - 1, p],
            ).start()

        @pl.when(jnp.logical_not(is_self(group)))
        def _():
            wts_copy(group).start()

        return carry

    def give():
        def turned(group):
            far = jnp.where(group < 4, 1 - bit, bit)
            return 2 * lax.rem(p + 2 + lax.rem(group, 4), 4) + far

        lax.fori_loop(0, GROUPS, lambda n, carry: give_pts(turned(n), carry), 0)
        lax.fori_loop(0, GROUPS, lambda n, carry: give_wts(turned(n), carry), 0)

    give()

    side_team = jnp.where(dl == 3, q + 1, q - 1)
    side_core = jnp.where(
        dl == 3,
        jnp.where(side_team < TEAMS // 2, 1, 0),
        jnp.where(side_team < TEAMS // 2, 0, 1),
    )

    def side_copy(group):
        return pts_copy(group, side_team, side_core, 0, ss_i.at[group])

    mate = d - 1

    def pts_pass(place):
        return remote(
            pts.at[place], pts.at[5 - place], ss_f.at[place - 1], rs_p.at[5 - place, 0], mate, p
        )

    def wts_pass(index):
        return remote(
            wts.at[index], wts.at[3 - index], ss_g.at[index], rs_w.at[3 - index, 0], mate, p
        )

    def wait_blocks(place):
        def one(k, carry):
            dst = pts.at[place, :, pl.ds(pl.multiple_of(k * 512, 512), 512)]
            remote(pts_in.at[0], dst, ss_u, rs_p.at[place, k], d, p).wait_recv()
            return carry

        lax.fori_loop(0, 4, one, 0)

    def take_pts(n):
        @pl.when(early)
        def _():
            wait_blocks(n)
            pts_pass(n).start()

        @pl.when(jnp.logical_not(early))
        def _():
            place = 5 - n
            remote(pts.at[place], pts.at[place], ss_u, rs_p.at[place, 0], d, p).wait_recv()

    def take_wts(n):
        @pl.when(early)
        def _():
            def one(k, carry):
                dst = wts.at[n - 1, :, pl.ds(pl.multiple_of(k * 512, 512), 512)]
                src = wsrc.at[pl.ds(0, 8), :]
                remote(src, dst, ss_u, rs_w.at[n - 1, k], d, p).wait_recv()
                return carry

            lax.fori_loop(0, 4, one, 0)
            wts_pass(n - 1).start()

        @pl.when(jnp.logical_not(early))
        def _():
            index = 4 - n
            remote(wts.at[index], wts.at[index], ss_u, rs_w.at[index, 0], d, p).wait_recv()

    def send_form(values):
        return jnp.concatenate([values[:, 0:1024], values[:, 1024:2048]], axis=0).astype(BF16)

    def advance(sent, index, sums, place=None):
        place = index if place is None else place
        weight = wts[place]
        live = (weight > 0.0).astype(F32)
        count = jnp.sum(live, axis=1, keepdims=True)
        if sums:
            row = rsum[index]
            each = jnp.concatenate(
                [
                    jnp.sum(sent[0:8].astype(F32) * row[:, 0:1024], axis=1, keepdims=True),
                    jnp.sum(sent[8:16].astype(F32) * row[:, 1024:2048], axis=1, keepdims=True),
                ],
                axis=0,
            )
            scale = count / (each[0:8] + each[8:16])
            scaled = live * scale
        out = []
        for n in range(4):
            at = slice(512 * n, 512 * n + 512)
            low_part = jnp.dot(sent, kern[index, 0:1024, at], preferred_element_type=F32)
            high_part = jnp.dot(sent, kern[index, 1024:2048, at], preferred_element_type=F32)
            got = low_part[0:8] + high_part[8:16]
            out.append(got * (scaled if sums else live)[:, at])
        if not sums:
            scale = count / sum(jnp.sum(part, axis=1, keepdims=True) for part in out)
            out = [part * scale for part in out]
        for n in range(4):
            res[place, :, 512 * n : 512 * n + 512] = out[n]
            out[n] = out[n] * weight[:, 512 * n : 512 * n + 512]
        return jnp.concatenate(
            [jnp.concatenate([out[n], out[n + 2]], axis=0).astype(BF16) for n in range(2)], axis=1
        )

    take_pts(1)
    take_pts(2)

    @pl.when(to_next | to_last)
    def _():
        def give_side(group, carry):
            side_copy(group).start()
            return carry

        lax.fori_loop(0, GROUPS, give_side, 0)

    quick = stage <= 1
    helps = stage == TEAMS - 1
    ask = remote(msg, alt, ss_h, rs_h, mate, p)
    reply = remote(turn, alt, ss_h, rs_h, d + 1, p)
    reply_res = remote(res.at[1], res.at[2], ss_k, rs_k, d + 1, p)

    def make_kernel(t, carry):
        index = jnp.where((t == 3) | (t < 0), 0, jnp.where(early, t + 1, 3 - t))

        first = t < 0
        paired = starts | helps

        @pl.when(((t == 1) & jnp.logical_not(paired)) | (t == 2))
        def _():
            take_pts(t + 2)

        @pl.when(jnp.logical_not(paired) & (t == 0))
        def _():
            take_wts(1)

        @pl.when((jnp.logical_not(paired) & (t < 3)) | (helps & (t == 2)))
        def _():
            take_wts(t + 2)

        @pl.when(first)
        def _():
            take_pts(3)
            for n in range(1, 4):
                take_wts(n)

        @pl.when(jnp.logical_not(starts) | (t == 0) | (t == 2))
        def _():
            @pl.when(t == 3)
            def _():
                wait_blocks(0)

            fill_side(left, pts[jnp.where(first, 3, index)], 1.0, True)
            fill_side(right, pts[jnp.where(first, 2, index + 1)], 2.0, False)

            def rows(r, inner):
                for c in range(ROWS // PART):
                    at = pl.ds(pl.multiple_of(r * ROWS + PART * c, PART), PART)
                    power = lax.dot_general(
                        left[:, at],
                        right[...],
                        (((0,), (0,)), ((), ())),
                        preferred_element_type=F32,
                    )
                    kern[index, at, :] = jnp.exp(power).astype(BF16)
                return inner

            def rows_summed(r, inner):
                at = pl.ds(pl.multiple_of(r * ROWS_SUMMED, ROWS_SUMMED), ROWS_SUMMED)
                power = lax.dot_general(
                    left[:, at], right[...], (((0,), (0,)), ((), ())), preferred_element_type=F32
                )
                values = jnp.exp(power).astype(BF16)
                kern[index, at, :] = values
                live = (wts[index, 0:1, :] > 0.0).astype(F32)
                part = jnp.zeros((ROWS_SUMMED, 128), F32)
                for c in range(16):
                    cut = slice(128 * c, 128 * c + 128)
                    part = part + values[:, cut].astype(F32) * live[:, cut]
                rsum[index, :, at] = jnp.concatenate(
                    [
                        jnp.sum(jnp.transpose(part[128 * c : 128 * c + 128]), axis=0, keepdims=True)
                        for c in range(ROWS_SUMMED // 128)
                    ],
                    axis=1,
                )
                return inner

            @pl.when(quick | first)
            def _():
                lax.fori_loop(0, 2048 // ROWS, rows, 0)

            @pl.when(jnp.logical_not(quick | first))
            def _():
                lax.fori_loop(0, 2048 // ROWS_SUMMED, rows_summed, 0)

        @pl.when(starts & (t == 0))
        def _():
            take_pts(3)
            for n in range(1, 4):
                take_wts(n)
            weight = wts[0]
            live = (weight > 0.0).astype(F32)
            res[0] = live
            msg[...] = send_form(live * weight)

        @pl.when(starts & (t == 2))
        def _():
            take_wts(4)
            ask.wait_send()
            ask.wait_recv()
            reply_res.wait_recv()
            msg[...] = alt[...]

        @pl.when(first)
        def _():
            ask.wait_recv()
            turn[...] = alt[...]

        @pl.when((starts & ((t == 0) | (t == 2))) | first)
        def _():
            @pl.when(first)
            def _():
                turn[...] = advance(turn[...], 0, False, 1)
                reply.start()
                reply_res.start()
                reply.wait_send()
                reply_res.wait_send()

            @pl.when(starts)
            def _():
                msg[...] = advance(msg[...], index, False)

            @pl.when(starts & (t == 0))
            def _():
                ask.start()

        return carry

    lax.fori_loop(jnp.where(helps, -1, 0), 4, make_kernel, 0)

    def make_fit():
        fill_side(left, pts[jnp.where(fwd, dl + 1, 4 - dl)], 1.0, True)
        fill_side(right, cells_in[0], 2.0, False)

        def rows(r, inner):
            at = pl.ds(pl.multiple_of(r * ROWS_SUMMED, ROWS_SUMMED), ROWS_SUMMED)
            power = lax.dot_general(
                left[:, at], right[...], (((0,), (0,)), ((), ())), preferred_element_type=F32
            )
            fit[at, :] = jnp.exp(power)
            return inner

        lax.fori_loop(0, 2048 // ROWS_SUMMED, rows, 0)

    next_team = jnp.where(fwd, q + 1, q - 1)
    next_core = jnp.where(fwd == (next_team < TEAMS // 2), 1, 0)
    next_day = 4 * next_team + 2 * (1 - xb) + next_core
    hop = remote(msg, msg, ss_u, rs_u, next_day, p)

    def cross(index):
        return remote(res.at[index], oth.at[3 - index], ss_x.at[index], rs_x.at[3 - index], mate, p)

    @pl.when(jnp.logical_not(early))
    def _():
        make_fit()

    @pl.when(jnp.logical_not(starts))
    def _():
        remote(msg, msg, ss_u, rs_u, d, p).wait_recv()

        @pl.when(quick)
        def _():
            def one(index, carry):
                msg[...] = advance(msg[...], index, False)
                return carry

            lax.fori_loop(0, 4, one, 0)

        @pl.when(jnp.logical_not(quick))
        def _():
            sent = msg[...]
            for index in range(4):
                sent = advance(sent, index, True)
            msg[...] = sent

    @pl.when(stage < TEAMS - 1)
    def _():
        hop.start()

    def mass_copy(index, k):
        return remote(
            mps.at[index], mbuf.at[g], ss_m.at[index, k], rs_m.at[g], day_at(index + 1), k
        )

    def here(index, k):
        return (day_at(index + 1) == d) & (k == p)

    @pl.when(jnp.logical_not(early))
    def _():
        def one(t, carry):
            index = 3 - t
            remote(res.at[index], oth.at[index], ss_u, rs_x.at[index], d, p).wait_recv()
            mps[index] = jnp.sum(res[index] * wts[index] * oth[index], axis=0, keepdims=True)

            def to(k, inner):
                @pl.when(here(index, k))
                def _():
                    pltpu.make_async_copy(mps.at[index], mbuf.at[g], rs_m.at[g]).start()

                @pl.when(jnp.logical_not(here(index, k)))
                def _():
                    mass_copy(index, k).start()

                return inner

            lax.fori_loop(0, 4, to, 0)
            return carry

        lax.fori_loop(0, 4, one, 0)

    @pl.when(early)
    def _():
        def one(index, carry):
            cross(index).start()
            return carry

        lax.fori_loop(0, 4, one, 0)

    way = jnp.where(fwd, 0, 1)
    rows_g = pl.ds(pl.multiple_of(8 * g, 8), 8)

    def out_copy(index, k):
        return remote(
            res.at[index, :, pl.ds(pl.multiple_of(k * 512, 512), 512)],
            fb_out.at[way, rows_g, :],
            ss_o.at[index, k],
            rs_o.at[way, g],
            day_at(index + 1),
            k,
        )

    def out_days(index, carry):
        def to(k, inner):
            @pl.when(here(index, k))
            def _():
                pltpu.make_async_copy(
                    res.at[index, :, pl.ds(pl.multiple_of(k * 512, 512), 512)],
                    fb_out.at[way, rows_g, :],
                    rs_o.at[way, g],
                ).start()

            @pl.when(jnp.logical_not(here(index, k)))
            def _():
                out_copy(index, k).start()

            return inner

        lax.fori_loop(0, 4, to, 0)
        return carry

    lax.fori_loop(0, 4, out_days, 0)

    @pl.when(early)
    def _():
        make_fit()

    def wait_mass(k, carry):
        remote(mps.at[0], mbuf.at[k], ss_u, rs_m.at[k], d, p).wait_recv()
        return carry

    lax.fori_loop(0, GROUPS, wait_mass, 0)
    mass = mbuf[0]
    for k in range(1, GROUPS):
        mass = mass + mbuf[k]
    mass_total = jnp.sum(mass, axis=1, keepdims=True)
    mrow[...] = jnp.zeros_like(mrow)
    for k in range(16):
        mrow[k : k + 1, :] = mass[:, 128 * k : 128 * k + 128]
    columns = jnp.transpose(mrow[...])
    total = jnp.zeros((8, 2048), F32)
    for k in range(16):
        block = fit[128 * k : 128 * k + 128, :] * columns[:, k : k + 1]
        total = total + jnp.sum(block.reshape(16, 8, 2048), axis=0)
    density = jnp.sum(total, axis=0, keepdims=True) / mass_total
    cell = lax.broadcasted_iota(jnp.int32, (1, 2048), 1) + p * 2048
    inverse = (cell < cc_in[0]).astype(F32) / density
    for k in range(16):
        part = jnp.zeros((128, 128), F32)
        for c in range(16):
            part = part + (
                fit[128 * k : 128 * k + 128, 128 * c : 128 * c + 128]
                * inverse[:, 128 * c : 128 * c + 128]
            )
        rpart[k // 4, :, 128 * (k % 4) : 128 * (k % 4) + 128] = jnp.sum(
            jnp.transpose(part), axis=0, keepdims=True
        )

    def ratio_copy(k):
        return remote(rpart.at[k], rbuf.at[p], ss_r.at[k], rs_r.at[p], d, k)

    def ratio_to(k, carry):
        @pl.when(k == p)
        def _():
            pltpu.make_async_copy(rpart.at[k], rbuf.at[p], rs_r.at[p]).start()

        @pl.when(k != p)
        def _():
            ratio_copy(k).start()

        return carry

    lax.fori_loop(0, 4, ratio_to, 0)

    def close_give(group, carry):
        @pl.when(jnp.logical_not(is_self(group)))
        def _():
            pts_copy(group, q, 1, place_own, ss_p.at[group]).wait_send()
            wts_copy(group).wait_send()

        @pl.when(to_next | to_last)
        def _():
            side_copy(group).wait_send()

        def arrived(way_in, inner):
            remote(
                res.at[0, :, pl.ds(0, 512)],
                fb_out.at[way_in, pl.ds(pl.multiple_of(8 * group, 8), 8), :],
                ss_u,
                rs_o.at[way_in, group],
                d,
                p,
            ).wait_recv()
            return inner

        lax.fori_loop(0, 2, arrived, 0)
        return carry

    lax.fori_loop(0, GROUPS, close_give, 0)

    def close_four(index, carry):
        @pl.when(early)
        def _():
            pts_pass(index + 1).wait_send()
            wts_pass(index).wait_send()
            cross(index).wait_send()

        def to(k, inner):
            @pl.when(jnp.logical_not(here(index, k)))
            def _():
                out_copy(index, k).wait_send()

                @pl.when(jnp.logical_not(early))
                def _():
                    mass_copy(index, k).wait_send()

            return inner

        lax.fori_loop(0, 4, to, 0)
        return carry

    lax.fori_loop(0, 4, close_four, 0)

    @pl.when(stage < TEAMS - 1)
    def _():
        hop.wait_send()

    def ratio_wait(k, carry):
        remote(rpart.at[0], rbuf.at[k], ss_u, rs_r.at[k], d, p).wait_recv()
        return carry

    lax.fori_loop(0, 4, ratio_wait, 0)
    summed = rbuf[0] + rbuf[1] + rbuf[2] + rbuf[3]
    fit_out[...] = summed

    def close_ratio(k, carry):
        @pl.when(k != p)
        def _():
            ratio_copy(k).wait_send()

        return carry

    lax.fori_loop(0, 4, close_ratio, 0)


def shards(points, cells, clone_weight, potential, support_count, cell_count):
    vmem = pl.BlockSpec(memory_space=pltpu.VMEM)
    smem = pl.BlockSpec(memory_space=pltpu.SMEM)
    dma = pltpu.SemaphoreType.DMA
    both, summed = pl.pallas_call(
        body,
        out_shape=(
            jax.ShapeDtypeStruct((2, 64, 512), F32),
            jax.ShapeDtypeStruct((1, 512), F32),
        ),
        in_specs=[vmem, vmem, vmem, vmem, smem, smem],
        out_specs=(pl.BlockSpec(memory_space=pl.ANY), vmem),
        scratch_shapes=[
            pltpu.VMEM((4, 2048, 2048), BF16),
            pltpu.VMEM((4, 1, 2048), F32),
            pltpu.VMEM((2048, 2048), F32),
            pltpu.VMEM((5, 64, 2048), BF16),
            pltpu.VMEM((4, 8, 2048), F32),
            pltpu.VMEM((4, 8, 2048), F32),
            pltpu.VMEM((4, 8, 2048), F32),
            pltpu.VMEM((16, 1024), BF16),
            pltpu.VMEM((16, 1024), BF16),
            pltpu.VMEM((16, 1024), BF16),
            pltpu.VMEM((64, 512), F32),
            pltpu.VMEM((DEPTH, 2048), BF16),
            pltpu.VMEM((DEPTH, 2048), BF16),
            pltpu.VMEM((4, 1, 2048), F32),
            pltpu.VMEM((GROUPS, 1, 2048), F32),
            pltpu.VMEM((128, 128), F32),
            pltpu.VMEM((4, 1, 512), F32),
            pltpu.VMEM((4, 1, 512), F32),
            dma((5, 4)),
            dma((4, 4)),
            dma((GROUPS,)),
            dma((GROUPS,)),
            dma((GROUPS,)),
            dma((4,)),
            dma((4,)),
            dma,
            dma,
            dma((2, GROUPS)),
            dma((4, 4)),
            dma((4,)),
            dma((4,)),
            dma((GROUPS,)),
            dma((4, 4)),
            dma((4,)),
            dma((4,)),
            dma,
            dma,
            dma,
            dma,
        ],
        compiler_params=pltpu.CompilerParams(
            collective_id=0, has_side_effects=True, vmem_limit_bytes=62 * 1024 * 1024
        ),
        name="days",
    )(points, cells, clone_weight, potential, support_count, cell_count)
    slot = jnp.arange(512, dtype=jnp.int32)[None] + lax.axis_index("pt") * 512
    live = (slot < support_count[0]).astype(F32)
    return both[0][None], both[1][None], live / cell_count[0].astype(F32) * summed


def solution(mesh):
    in_specs = (
        P("day", None, "pt"),
        P("day", None, "pt"),
        P("day", None, "pt"),
        P("day", "pt"),
        P("day"),
        P("day"),
    )
    out_specs = (P("day", None, "pt"), P("day", None, "pt"), P("day", "pt"))
    return jax.shard_map(shards, mesh=mesh, in_specs=in_specs, out_specs=out_specs, check_vma=False)
```
